512 devices in a mesh: island: 8 (over y_lo, core), fsdp: 64 (over x, y_hi, z).
Axes of the slice: x: 4, y: 8 (y_hi: 2, y_lo: 4; y = y_hi * 4 + y_lo), z: 8, core: 2. Of those that a mesh axis runs over, the one named last changes fastest.
Arguments:
- features: bfloat16 [2, 8, 16384, 4096], P(None, 'island', 'fsdp'), may hold values from -6 to 6
- targets: bfloat16 [2, 8, 16384, 128], P(None, 'island', 'fsdp'), may hold values from -6 to 6
- labels: int32 [2, 8, 16384], P(None, 'island', 'fsdp'), may hold values from -100 to 128255
- fragment: int32 [1], replicated, may hold values from 0 to 4095
- local_weight: float32 [8, 4096, 128], P('island', 'fsdp'), may hold values from -0.09375 to 0.09375
- inner_velocity: float32 [8, 4096, 128], P('island', 'fsdp'), may hold values from -0.09375 to 0.09375
- global_weight: float32 [4096, 128], P('fsdp'), may hold values from -0.09375 to 0.09375
- outer_velocity: float32 [4096, 128], P('fsdp'), may hold values from -0.09375 to 0.09375
Outputs:
- local_out: float32 [8, 4096, 128], P('island', 'fsdp')
- velocity_out: float32 [8, 4096, 128], P('island', 'fsdp')
- global_out: float32 [4096, 128], P('fsdp')
- outer_out: float32 [4096, 128], P('fsdp')
- predictions: bfloat16 [8, 16384, 128], P('island', 'fsdp')
The draws below stay inside these ranges and needn't reach their ends.
All inputs are finite; a program needn't handle non-finite values.
Results may differ from the reference program's by a relative error of at most 0.015.
Values may be sent and summed in bfloat16 or wider, within the bound.
A program may use at most 64 MiB of HBM per device.

```python
import jax
import jax.numpy as jnp
from jax import lax

D = 4096
E = 128
VOCAB = 128256
FRAG = 16
FBLK = 4
STEPS = 2
ISL = 8
TOK_ISL = 16384


def draw_labels(key, part):
    key = jax.random.fold_in(key, 11)
    first, second = jax.random.split(key)
    token_ids = jax.random.randint(first, (STEPS, ISL, TOK_ISL), 0, VOCAB)
    coins = jax.random.randint(second, (STEPS, ISL, TOK_ISL), 0, 1000)
    position = lax.broadcasted_iota(jnp.int32, (STEPS, ISL, TOK_ISL), 2)
    step_index = lax.broadcasted_iota(jnp.int32, (STEPS, ISL, TOK_ISL), 0)
    island_index = lax.broadcasted_iota(jnp.int32, (STEPS, ISL, TOK_ISL), 1)
    corner = (position == 0) & (step_index == 0) & (island_index == 0)
    token_ids = jnp.where(corner, VOCAB - 1, token_ids)
    limit = 280 + 570 * position // TOK_ISL
    retained = (coins < limit) | (position == 0)
    return jnp.where(retained, token_ids, -100).astype(jnp.int32)


def levels(stream_key, dims, cuts, low, high):
    factor_of = 1.0
    for dim, shards_of in cuts:
        heights = jax.random.uniform(jax.random.fold_in(jax.random.fold_in(stream_key, 6), dim), (shards_of,), jnp.float32, low / len(cuts), high / len(cuts))
        factor_of = factor_of * jnp.repeat(jnp.exp(heights), dims[dim] // shards_of).reshape((-1,) + (1,) * (len(dims) - 1 - dim))
    return factor_of


def noise(stream_key, dims, scale, bound, cuts=(), held_as=jnp.bfloat16):
    values = jax.random.normal(stream_key, dims, jnp.float32) * scale
    if len(cuts) > 0:
        values = levels(stream_key, dims, cuts, -0.22, 0.18) * values
    return jnp.clip(values, min=-bound, max=bound).astype(held_as)


def setup_inputs(seed: int = 0) -> dict:
    streams_of = jax.random.split(jax.random.key(seed), 9)
    return {
        "features": noise(streams_of[0], (STEPS, ISL, TOK_ISL, D), 1.0, 6.0, ((1, 8), (2, 64))),
        "targets": noise(streams_of[1], (STEPS, ISL, TOK_ISL, E), 1.0, 6.0, ((1, 8), (2, 64))),
        "labels": draw_labels(jax.random.fold_in(streams_of[8], 71), 0),
        "fragment": jax.random.randint(streams_of[3], (1,), 0, 4096).astype(jnp.int32),
        "local_weight": noise(streams_of[4], (ISL, D, E), D ** -0.5, 0.09375, ((0, 8), (1, 64)), jnp.float32),
        "inner_velocity": noise(streams_of[5], (ISL, D, E), D ** -0.5, 0.09375, ((0, 8), (1, 64)), jnp.float32),
        "global_weight": noise(streams_of[6], (D, E), D ** -0.5, 0.09375, ((0, 64),), jnp.float32),
        "outer_velocity": noise(streams_of[7], (D, E), D ** -0.5, 0.09375, ((0, 64),), jnp.float32),
    }


INNER_RATE = 0.3
INNER_MOMENTUM = 0.9
OUTER_RATE = 0.7
OUTER_MOMENTUM = 0.9
MERGE_WEIGHT = 0.5


def as_blocks(array):
    return array.reshape(array.shape[0] // (FBLK * FRAG), FRAG, FBLK, array.shape[-1])


def select_rows(array, chosen):
    return lax.dynamic_slice_in_dim(as_blocks(array), chosen, 1, 1)


def place_rows(array, rows, chosen):
    return lax.dynamic_update_slice_in_dim(as_blocks(array), rows, chosen, 1).reshape(array.shape)


def inner_step(weight, velocity, features, targets, labels):
    retained = (labels >= 0).astype(jnp.float32)
    total = jnp.sum(retained)
    predicted = jnp.dot(features, weight.astype(jnp.bfloat16), preferred_element_type=jnp.float32)
    errors = (retained[:, None] * (predicted - targets.astype(jnp.float32))).astype(jnp.bfloat16)
    gradient = lax.dot_general(features, errors, (((0,), (0,)), ((), ())), preferred_element_type=jnp.float32) / total
    velocity = INNER_MOMENTUM * velocity + gradient
    return weight - INNER_RATE * velocity, velocity, predicted


def reference(features, targets, labels, fragment, local_weight, inner_velocity, global_weight, outer_velocity):
    chosen = (fragment[0] % FRAG).astype(jnp.int32)
    start_rows = select_rows(global_weight, chosen)
    summed = jnp.zeros_like(start_rows)
    for island in range(ISL):
        summed = summed + (start_rows - select_rows(local_weight[island], chosen))
    outer_mean = summed / ISL
    outer_rows = OUTER_MOMENTUM * select_rows(outer_velocity, chosen) + outer_mean
    global_rows = start_rows - OUTER_RATE * (OUTER_MOMENTUM * outer_rows + outer_mean)
    local_list = []
    velocity_list = []
    predicted_list = []
    for island in range(ISL):
        weight, velocity, unused = inner_step(local_weight[island], inner_velocity[island], features[0, island], targets[0, island], labels[0, island])
        merged = MERGE_WEIGHT * global_rows + (1.0 - MERGE_WEIGHT) * select_rows(weight, chosen)
        weight = place_rows(weight, merged, chosen)
        weight, velocity, predicted = inner_step(weight, velocity, features[1, island], targets[1, island], labels[1, island])
        local_list.append(weight)
        velocity_list.append(velocity)
        predicted_list.append(predicted)
    return (jnp.stack(local_list), jnp.stack(velocity_list), place_rows(global_weight, global_rows, chosen), place_rows(outer_velocity, outer_rows, chosen), jnp.stack(predicted_list).astype(jnp.bfloat16))
```

```python
import functools

import jax
import jax.numpy as jnp
from jax import lax
from jax.experimental import pallas as pl
from jax.experimental.pallas import tpu as pltpu
from jax.sharding import PartitionSpec as P

FRAG = 16
FBLK = 4

INNER_RATE = 0.3
INNER_MOMENTUM = 0.9
OUTER_RATE = 0.7
OUTER_MOMENTUM = 0.9
MERGE_WEIGHT = 0.5

NX, NY, NZ = 4, 2, 8
MESH = pl.DeviceIdType.MESH


def near_first(i):
    h = i // 2 + 1
    return h + (i % 2) * (NZ - 2 * h)


def far_first(i):
    return near_first(NZ - 2 - i)


def kernel(
    islands,
    frag_ref, feat_ref, tgt_ref, lab_ref, w_ref, v_ref, gw_ref, ov_ref,
    w_out, v_out, g_out, o_out, p_out,
    xbuf, wg, grad, gb, rx, sz, rz, sy, ry, cbuf, cz, cx, cy, dbuf, dz, keep,
    feat_sem, zs, zr, xs, xr, ys, yr, bxs, bxr, bzs, bzr, bys, byr,
    czs, czr, cxs, cxr, cys, cyr, ds_, dr,
):
    f32, bf16 = jnp.float32, jnp.bfloat16
    f = lax.axis_index("fsdp")
    isl = lax.axis_index("island")
    x, y, z = f // (NY * NZ), (f // NZ) % NY, f % NZ
    other = 1 - y

    def dev(dx=0, dy=0, dz_=0):
        return {"fsdp": (((x + dx) % NX) * NY + (y + dy) % NY) * NZ + (z + dz_) % NZ}

    def peer(i):
        return {"island": (isl + i) % islands}

    def remote(src, dst, ss, rs, to):
        return pltpu.make_async_remote_copy(src, dst, ss, rs, device_id=to, device_id_type=MESH)

    def loop(n, body, start=0):
        def step(i, c):
            body(i)
            return c
        lax.fori_loop(start, n, step, 0)

    feats = [pltpu.make_async_copy(feat_ref.at[s, 0], xbuf.at[s], feat_sem.at[s]) for s in range(2)]
    for c in feats:
        c.start()

    barrier = pltpu.get_barrier_semaphore()

    def greet(to):
        pl.semaphore_signal(barrier, inc=1, device_id=to, device_id_type=MESH)

    loop(NZ, lambda d: greet(dev(dz_=d)), 1)
    loop(NX, lambda d: greet(dev(dx=d)), 1)
    greet(dev(dy=1))
    loop(islands, lambda i: greet(peer(i)), 1)

    wg[0, x, y, z] = w_ref[0].astype(bf16)
    retained = [(lab_ref[s] >= 0).astype(f32) for s in range(2)]
    halves = [r[:, :128] + r[:, 128:] for r in retained]
    row8 = lax.broadcasted_iota(jnp.int32, (8, 128), 0)
    cbuf[0] = jnp.where(row8 == 0, halves[0], jnp.where(row8 == 1, halves[1], 0.0))
    chosen = frag_ref[0] & (FRAG - 1)
    rows = lax.broadcasted_iota(jnp.int32, (64, 128), 0)
    mine = (rows // FBLK) == chosen
    diff = jnp.where(mine, gw_ref[...] - w_ref[0], 0.0)
    dbuf[...] = jnp.sum(diff.reshape(8, 8, 128), axis=0)

    pl.semaphore_wait(barrier, (NZ - 1) + (NX - 1) + 1 + (islands - 1))

    def which(k):
        return (y + k) % NY

    def ag_y(s):
        blk = wg.at[s, x, y, z]
        return remote(blk, blk, ys.at[s], yr.at[s], dev(dy=1))

    def ag_z(s, k, d):
        blk = wg.at[s, x, which(k), z]
        return remote(blk, blk, zs.at[s, k, d], zr.at[s, k, d], dev(dz_=d))

    def ag_x(s, k, d, dx):
        blk = wg.at[s, x, which(k), (z + NZ - d) % NZ]
        return remote(blk, blk, xs.at[s, k, d, dx], xr.at[s, k, d, dx], dev(dx=dx))

    def ag_open(s, k):
        loop(NZ - 1, lambda i: ag_z(s, k, far_first(i)).start())
        for dx in (2, 1, 3):
            ag_x(s, k, 0, dx).start()

    def ag_pass(s, k, lo, hi):
        def body(i):
            d = near_first(i)
            ag_z(s, k, d).wait_recv()
            for dx in (2, 1, 3):
                ag_x(s, k, d, dx).start()
        loop(hi, body, lo)

    def ag_wait(s, k):
        def body(d):
            for dx in (1, 3, 2):
                ag_x(s, k, d, dx).wait_recv()
        loop(NZ, body)

    def ag_begin(s):
        ag_y(s).start()
        ag_open(s, 0)

    def ag_middle(s):
        ag_pass(s, 0, 0, 4)
        ag_y(s).wait_recv()
        ag_open(s, 1)
        ag_pass(s, 0, 4, NZ - 1)
        ag_pass(s, 1, 0, NZ - 1)

    def count_z(d):
        return remote(cbuf.at[0], cz.at[d], czs.at[d], czr.at[d], dev(dz_=d))

    def count_x(d):
        return remote(cbuf.at[1], cx.at[d], cxs.at[d], cxr.at[d], dev(dx=d))

    def count_y():
        return remote(cbuf.at[2], cy, cys, cyr, dev(dy=1))

    def outer(i):
        return remote(dbuf, dz.at[i], ds_.at[i], dr.at[i], peer(i))

    def rs_x(s, k, d, dx):
        zz = (z + d) % NZ
        return remote(
            gb.at[s, (x + dx) % NX, which(k), zz], rx.at[s, k, d, dx],
            bxs.at[s, k, d, dx], bxr.at[s, k, d, dx], dev(dx=dx),
        )

    def rs_z(s, k, d):
        return remote(sz.at[s, k, d], rz.at[s, k, d], bzs.at[s, k, d], bzr.at[s, k, d], dev(dz_=d))

    def rs_y(s):
        return remote(sy.at[s], ry.at[s], bys.at[s], byr.at[s], dev(dy=1))

    def columns(xx, yy):
        return pl.ds(pl.multiple_of((xx * NY + yy) * (NZ * 64), NZ * 64), NZ * 64)

    def forward(s, k, acc):
        def body(xx, acc):
            yy = which(k)
            piece = wg[s, xx, yy].reshape(NZ * 64, 128)
            return acc + jnp.dot(xbuf[s, :, columns(xx, yy)], piece, preferred_element_type=f32)
        return lax.fori_loop(0, NX, body, acc)

    def reduce(s, errors):
        for k in (1, 0):
            def block(i):
                dx = (NX + 2 - i) % NX
                xx, yy = (x + dx) % NX, which(k)
                part = lax.dot_general(
                    xbuf[s, :, columns(xx, yy)], errors, (((0,), (0,)), ((), ())),
                    preferred_element_type=f32,
                ).reshape(NZ, 64, 128)
                return dx, xx, yy, part

            for i in (0, 1, 3):
                dx, xx, yy, part = block(i)
                gb[s, xx, yy] = part.astype(bf16)
                loop(NZ - 1, lambda j: rs_x(s, k, far_first(j), dx).start())
                rs_x(s, k, 0, dx).start()
            dx, xx, yy, part = block(2)
            grad[k] = part
        for k in (1, 0):
            def total(d):
                for dx in (1, 3, 2):
                    rs_x(s, k, d, dx).wait_recv()
                t = grad[k, (z + d) % NZ]
                for dx in (1, 2, 3):
                    t = t + rx[s, k, d, dx].astype(f32)
                return t

            def body(j):
                d = far_first(j)
                sz[s, k, d] = total(d).astype(bf16)
                rs_z(s, k, d).start()
            loop(NZ - 1, body)
            keep[k] = total(0)

        def plane(k):
            def body(d, t):
                rs_z(s, k, d).wait_recv()
                return t + rz[s, k, d].astype(f32)
            return lax.fori_loop(1, NZ, body, keep[k])
        sy[s] = plane(1).astype(bf16)
        rs_y(s).start()
        t = plane(0)
        rs_y(s).wait_recv()
        return t + ry[s].astype(f32)

    def mask_of(s):
        return jnp.broadcast_to(retained[s], (128, 256)).T

    def errors_of(s, predicted):
        return (mask_of(s) * (predicted - tgt_ref[s, 0].astype(f32))).astype(bf16)

    ag_begin(0)
    loop(islands, lambda i: outer(i).start(), 1)
    loop(NZ, lambda d: count_z(d).start(), 1)
    ag_middle(0)

    def count_sum(d, t):
        count_z(d).wait_recv()
        return t + cz[d]
    cbuf[1] = lax.fori_loop(1, NZ, count_sum, cbuf[0])
    loop(NX, lambda d: count_x(d).start(), 1)

    feats[0].wait()
    ag_wait(0, 0)
    acc = forward(0, 0, jnp.zeros((256, 128), f32))

    def count_sum_x(d, t):
        count_x(d).wait_recv()
        return t + cx[d]
    cbuf[2] = lax.fori_loop(1, NX, count_sum_x, cbuf[1])
    count_y().start()

    ag_wait(0, 1)
    acc = forward(0, 1, acc)
    gradient = reduce(0, errors_of(0, acc))

    count_y().wait_recv()
    counts = cbuf[2] + cy[...]
    first_total = jnp.sum(jnp.where(row8 == 0, counts, 0.0))
    second_total = jnp.sum(jnp.where(row8 == 1, counts, 0.0))

    def outer_sum(i, t):
        outer(i).wait_recv()
        return t + dz[i]
    summed = lax.fori_loop(1, islands, outer_sum, dbuf[...])
    outer_mean = jnp.broadcast_to((summed / islands)[None], (8, 8, 128)).reshape(64, 128)
    outer_rows = OUTER_MOMENTUM * ov_ref[...] + outer_mean
    global_rows = gw_ref[...] - OUTER_RATE * (OUTER_MOMENTUM * outer_rows + outer_mean)
    g_out[...] = jnp.where(mine, global_rows, gw_ref[...])
    o_out[...] = jnp.where(mine, outer_rows, ov_ref[...])

    velocity = INNER_MOMENTUM * v_ref[0] + gradient / first_total
    weight = w_ref[0] - INNER_RATE * velocity
    weight = jnp.where(mine, MERGE_WEIGHT * global_rows + (1.0 - MERGE_WEIGHT) * weight, weight)
    wg[1, x, y, z] = weight.astype(bf16)

    ag_begin(1)
    v_out[0] = velocity
    w_out[0] = weight
    ag_middle(1)
    feats[1].wait()
    ag_wait(1, 0)
    acc = forward(1, 0, jnp.zeros((256, 128), f32))
    ag_wait(1, 1)
    acc = forward(1, 1, acc)
    p_out[0] = acc.astype(bf16)
    gradient = reduce(1, errors_of(1, acc))
    velocity = INNER_MOMENTUM * v_out[0] + gradient / second_total
    v_out[0] = velocity
    w_out[0] = w_out[0] - INNER_RATE * velocity

    for s in range(2):
        ag_y(s).wait_send()
        rs_y(s).wait_send()
        for k in range(2):
            def sent_z(d):
                ag_z(s, k, d).wait_send()
                rs_z(s, k, d).wait_send()
            loop(NZ, sent_z, 1)

            def sent_x(d):
                for dx in (1, 2, 3):
                    ag_x(s, k, d, dx).wait_send()
                    rs_x(s, k, d, dx).wait_send()
            loop(NZ, sent_x)
    loop(NZ, lambda d: count_z(d).wait_send(), 1)
    loop(NX, lambda d: count_x(d).wait_send(), 1)
    count_y().wait_send()
    loop(islands, lambda i: outer(i).wait_send(), 1)


def local(
    features, targets, labels, fragment, local_weight, inner_velocity, global_weight, outer_velocity
):
    islands = lax.axis_size("island")
    f32, bf16 = jnp.float32, jnp.bfloat16
    vmem = pl.BlockSpec(memory_space=pltpu.VMEM)
    dma, V = pltpu.SemaphoreType.DMA, pltpu.VMEM
    return pl.pallas_call(
        functools.partial(kernel, islands),
        out_shape=(
            jax.ShapeDtypeStruct((1, 64, 128), f32),
            jax.ShapeDtypeStruct((1, 64, 128), f32),
            jax.ShapeDtypeStruct((64, 128), f32),
            jax.ShapeDtypeStruct((64, 128), f32),
            jax.ShapeDtypeStruct((1, 256, 128), bf16),
        ),
        in_specs=[
            pl.BlockSpec(memory_space=pltpu.SMEM), pl.BlockSpec(memory_space=pl.ANY),
            vmem, vmem, vmem, vmem, vmem, vmem,
        ],
        out_specs=(vmem,) * 5,
        scratch_shapes=[
            V((2, 256, 4096), bf16),
            V((2, NX, NY, NZ, 64, 128), bf16),
            V((2, NZ, 64, 128), f32),
            V((2, NX, NY, NZ, 64, 128), bf16),
            V((2, 2, NZ, NX, 64, 128), bf16),
            V((2, 2, NZ, 64, 128), bf16),
            V((2, 2, NZ, 64, 128), bf16),
            V((2, 64, 128), bf16),
            V((2, 64, 128), bf16),
            V((3, 8, 128), f32),
            V((NZ, 8, 128), f32),
            V((NX, 8, 128), f32),
            V((8, 128), f32),
            V((8, 128), f32),
            V((islands, 8, 128), f32),
            V((2, 64, 128), f32),
            dma((2,)),
            dma((2, 2, NZ)), dma((2, 2, NZ)),
            dma((2, 2, NZ, NX)), dma((2, 2, NZ, NX)),
            dma((2,)), dma((2,)),
            dma((2, 2, NZ, NX)), dma((2, 2, NZ, NX)),
            dma((2, 2, NZ)), dma((2, 2, NZ)),
            dma((2,)), dma((2,)),
            dma((NZ,)), dma((NZ,)), dma((NX,)), dma((NX,)), dma, dma,
            dma((islands,)), dma((islands,)),
        ],
        compiler_params=pltpu.CompilerParams(
            collective_id=0, has_side_effects=True, vmem_limit_bytes=40 << 20
        ),
        cost_estimate=pl.CostEstimate(flops=1 << 30, bytes_accessed=5 << 20, transcendentals=0),
    )(fragment, features, targets, labels, local_weight, inner_velocity, global_weight, outer_velocity)


def solution(mesh):
    return jax.shard_map(
        local,
        mesh=mesh,
        in_specs=(
            P(None, "island", "fsdp", None),
            P(None, "island", "fsdp", None),
            P(None, "island", "fsdp"),
            P(),
            P("island", "fsdp", None),
            P("island", "fsdp", None),
            P("fsdp", None),
            P("fsdp", None),
        ),
        out_specs=(
            P("island", "fsdp", None),
            P("island", "fsdp", None),
            P("fsdp", None),
            P("fsdp", None),
            P("island", "fsdp", None),
        ),
        check_vma=False,
    )
```

```python
import functools

import jax
import jax.numpy as jnp
from jax import lax
from jax.experimental import pallas as pl
from jax.experimental.pallas import tpu as pltpu
from jax.sharding import PartitionSpec as P

FRAG = 16
FBLK = 4

INNER_RATE = 0.3
INNER_MOMENTUM = 0.9
OUTER_RATE = 0.7
OUTER_MOMENTUM = 0.9
MERGE_WEIGHT = 0.5

NX, NY, NZ = 4, 2, 8
MESH = pl.DeviceIdType.MESH


OFF = (0, 1, 7, 2, 6, 3, 5, 4)
GROUPS = ((0, 3), (3, 8))
STREAMS = 2
HALF = 64


def turned(a):
    return pltpu.roll(a, HALF, 1)


def kernel(
    islands,
    frag_ref, feat_hbm, tgt_hbm, lab_hbm, w_hbm, v_hbm, gw_hbm, ov_hbm,
    w_out, v_out, g_out, o_out, p_out,
    tgt_ref, lab_ref, w_ref, v_ref, gw_ref, ov_ref,
    xbuf, wg, piece, grad, gb, rx, sz, rz, sy, ry, cbuf, cz, cx, cy, dbuf, dz, keep,
    wf, vf, gf, mask, pred,
    load_sem, feat_sem, zs, zr, xs, xr, ys, yr, bxs, bxr, bzs, bzr, bys, byr,
    small_s, small_r,
):
    f32, bf16 = jnp.float32, jnp.bfloat16
    f = lax.axis_index("fsdp")
    isl = lax.axis_index("island")
    x, y, z = f // (NY * NZ), (f // NZ) % NY, f % NZ

    def dev(dx=0, dy=0, dz_=0):
        return {"fsdp": (((x + dx) % NX) * NY + (y + dy) % NY) * NZ + (z + dz_) % NZ}

    def peer(i):
        return {"island": (isl + i) % islands}

    def remote(src, dst, ss, rs, to):
        return pltpu.make_async_remote_copy(src, dst, ss, rs, device_id=to, device_id_type=MESH)

    def loop(n, body, start=0):
        def step(i, c):
            body(i)
            return c
        lax.fori_loop(start, n, step, 0)

    pairs = (
        (w_hbm, w_ref), (lab_hbm, lab_ref), (gw_hbm, gw_ref), (v_hbm, v_ref), (ov_hbm, ov_ref), (tgt_hbm, tgt_ref),
    )
    loads = [pltpu.make_async_copy(a, b, load_sem.at[i]) for i, (a, b) in enumerate(pairs)]
    feats = [pltpu.make_async_copy(feat_hbm.at[s, 0], xbuf.at[s], feat_sem.at[s]) for s in range(2)]

    barrier = pltpu.get_barrier_semaphore()

    def greet(to):
        pl.semaphore_signal(barrier, inc=1, device_id=to, device_id_type=MESH)

    loop(NZ, lambda d: greet(dev(dz_=d)), 1)
    loop(NX, lambda d: greet(dev(dx=d)), 1)
    greet(dev(dy=1))
    loop(islands, lambda i: greet(peer(i)), 1)
    for c in loads + feats:
        c.start()
    for c in loads:
        c.wait()

    lane32 = lax.broadcasted_iota(jnp.int32, (32, 128), 1)
    lane = lax.broadcasted_iota(jnp.int32, (256, 128), 1)

    def fold(a, c):
        low, high = a[:32], a[32:]
        if c == 0:
            return jnp.where(lane32 < HALF, low, turned(high))
        return jnp.where(lane32 < HALF, turned(low), high)

    def unfold(a, b):
        return jnp.concatenate([
            jnp.where(lane32 < HALF, a, turned(b)), jnp.where(lane32 < HALF, turned(a), b),
        ], axis=0)

    for c in range(STREAMS):
        wf[c] = fold(w_ref[0], c)
        wg[0, c, x, 0, 0] = wf[c].astype(bf16)
        vf[c] = fold(v_ref[0], c)
    retained = [(lab_ref[s] >= 0).astype(f32) for s in range(2)]
    halves = [r[:, :128] + r[:, 128:] for r in retained]
    row8 = lax.broadcasted_iota(jnp.int32, (8, 128), 0)
    cbuf[0] = jnp.where(row8 == 0, halves[0], jnp.where(row8 == 1, halves[1], 0.0))
    chosen = frag_ref[0] & (FRAG - 1)
    rows = lax.broadcasted_iota(jnp.int32, (64, 128), 0)
    mine = (rows // FBLK) == chosen
    rows32 = lax.broadcasted_iota(jnp.int32, (32, 128), 0) + jnp.where(lane32 < HALF, 0, 32)
    mine_folded = (rows32 // FBLK) == chosen
    diff = jnp.where(mine, gw_ref[...] - w_ref[0], 0.0)
    dbuf[...] = jnp.sum(diff.reshape(8, 8, 128), axis=0)

    pl.semaphore_wait(barrier, (NZ - 1) + (NX - 1) + 1 + (islands - 1))

    def which(k):
        return (y + k) % NY

    def ag_y(s, c):
        return remote(wg.at[s, c, x, 0, 0], wg.at[s, c, x, 1, 0], ys.at[c], yr.at[s, c], dev(dy=1))

    def ag_z(s, c, k, i):
        g = [lo <= i < hi for lo, hi in GROUPS].index(True)
        return remote(
            wg.at[s, c, x, k, 0], wg.at[s, c, x, k, i], zs.at[c, k], zr.at[s, c, k, g], dev(dz_=NZ - OFF[i])
        )

    def ag_x(s, c, k, g, dx):
        blk = wg.at[s, c, x, k, pl.ds(GROUPS[g][0], GROUPS[g][1] - GROUPS[g][0])]
        return remote(blk, blk, xs.at[c, k], xr.at[s, c, k], dev(dx=dx))

    def all_of(ref, ss, rs):
        return remote(ref, ref, ss, rs, dev(dx=1))

    def ag_open(s, c, k):
        for i in range(NZ - 1, 0, -1):
            ag_z(s, c, k, i).start()

    def ag_pass(s, c, k, groups=range(len(GROUPS))):
        for g in groups:
            lo, hi = GROUPS[g]
            first = max(lo, 1)
            if first < hi:
                all_of(wg.at[s, c, x, k, pl.ds(first, hi - first)], zs.at[c, k], zr.at[s, c, k, g]).wait_recv()
            for dx in (2, 1, 3):
                ag_x(s, c, k, g, dx).start()

    def ag_wait(s, c, k):
        all_of(wg.at[s, c, pl.ds(0, NX - 1), k], xs.at[c, k], xr.at[s, c, k]).wait_recv()

    def ag_begin(s, c):
        ag_y(s, c).start()
        ag_open(s, c, 0)

    def ag_turn(s, c):
        ag_y(s, c).wait_recv()
        ag_open(s, c, 1)

    def count_z(d):
        return remote(cbuf.at[0], cz.at[d], small_s.at[0], small_r.at[0], dev(dz_=d))

    def count_x(d):
        return remote(cbuf.at[1], cx.at[d], small_s.at[1], small_r.at[1], dev(dx=d))

    def count_y():
        return remote(cbuf.at[2], cy, small_s.at[2], small_r.at[2], dev(dy=1))

    def outer(i):
        return remote(dbuf, dz.at[i], small_s.at[3], small_r.at[3], peer(i))

    def all_small(j):
        ref, n = ((cz, NZ), (cx, NX), None, (dz, islands))[j]
        return all_of(ref.at[pl.ds(1, n - 1)], small_s.at[j], small_r.at[j])

    def rs_x(s, c, k, g, dx):
        part = pl.ds(GROUPS[g][0], GROUPS[g][1] - GROUPS[g][0])
        return remote(
            gb.at[s, c, (x + dx) % NX, k, part], rx.at[s, c, k, dx, part],
            bxs.at[c, k], bxr.at[s, c, k, g], dev(dx=dx),
        )

    def rs_z(s, c, k, i):
        return remote(sz.at[s, c, k, i], rz.at[s, c, k, i], bzs.at[c, k], bzr.at[s, c, k], dev(dz_=OFF[i]))

    def rs_y(s, c):
        return remote(sy.at[s, c], ry.at[s, c], bys.at[c], byr.at[s, c], dev(dy=1))

    def columns(xx, yy):
        return pl.ds(pl.multiple_of((xx * NY + yy) * (NZ * 64), NZ * 64), NZ * 64)

    def forward(s, c, k, acc):
        def body(xx, acc):
            for i in range(NZ):
                at = pl.multiple_of(((z + OFF[i]) % NZ) * 64, 64)
                block = wg[s, c, xx, k, i]
                piece[xx, pl.ds(at, 32)] = block
                piece[xx, pl.ds(at + 32, 32)] = turned(block.astype(f32)).astype(bf16)
            return acc + jnp.dot(xbuf[s, :, columns(xx, which(k))], piece[xx], preferred_element_type=f32)
        return lax.fori_loop(0, NX, body, acc)

    def spread(s, c, errors):
        for k in (1, 0):
            def block(dx):
                xx = (x + dx) % NX
                part = lax.dot_general(
                    xbuf[s, :, columns(xx, which(k))], errors, (((0,), (0,)), ((), ())),
                    preferred_element_type=f32,
                ).reshape(NZ, 2, 32, 128)
                low, high = part[:, 0].reshape(NZ * 32, 128), part[:, 1].reshape(NZ * 32, 128)
                folded = (low + turned(high)).reshape(NZ, 32, 128)
                for zz in range(NZ):
                    e = (zz - z + NZ) % NZ
                    slot = jnp.where(e == 0, 0, jnp.where(e <= NZ // 2, 2 * e - 1, 2 * (NZ - e)))
                    yield xx, slot, folded[zz]

            for dx in (2, 1, 3):
                for xx, slot, part in block(dx):
                    gb[s, c, xx, k, slot] = part.astype(bf16)
                for g in reversed(range(len(GROUPS))):
                    rs_x(s, c, k, g, dx).start()
            for _, slot, part in block(0):
                grad[c, k, slot] = part

    def gather_terms(s, c, k):
        for g in reversed(range(len(GROUPS))):
            lo, hi = GROUPS[g]
            part = rx.at[s, c, k, pl.ds(1, NX - 1), pl.ds(lo, hi - lo)]
            all_of(part, bxs.at[c, k], bxr.at[s, c, k, g]).wait_recv()
            t = grad[c, k, lo:hi]
            for dx in (1, 2, 3):
                t = t + rx[s, c, k, dx, lo:hi].astype(f32)
            sz[s, c, k, lo:hi] = t.astype(bf16)
            if lo == 0:
                keep[c, k] = t[0]
            for i in range(hi - 1, max(lo, 1) - 1, -1):
                rs_z(s, c, k, i).start()

    def plane(s, c, k):
        t = keep[c, k]
        all_of(rz.at[s, c, k, pl.ds(1, NZ - 1)], bzs.at[c, k], bzr.at[s, c, k]).wait_recv()
        for i in range(1, NZ):
            t = t + rz[s, c, k, i].astype(f32)
        return t

    def far_sum(s, c):
        sy[s, c] = plane(s, c, 1).astype(bf16)
        rs_y(s, c).start()

    def own_sum(s, c):
        t = plane(s, c, 0)
        rs_y(s, c).wait_recv()
        return t + ry[s, c].astype(f32)

    def errors_of(s, c, predicted):
        target = tgt_ref[s, 0].astype(f32)
        if c:
            target = turned(target)
        return jnp.where(lane < HALF, mask[s] * (predicted - target), 0.0).astype(bf16)

    def compute(s, c):
        acc = jnp.zeros((256, 128), f32)
        for k in range(2):
            ag_wait(s, c, k)
            acc = forward(s, c, k, acc)
        if s == 1:
            pred[c] = acc
        spread(s, c, errors_of(s, c, acc))

    def sent_gather(s, c):
        ag_y(s, c).wait_send()
        for k in range(2):
            all_of(wg.at[s, c, x, k, pl.ds(1, NZ - 1)], zs.at[c, k], zr.at[s, c, k, 0]).wait_send()
            all_of(wg.at[s, c, pl.ds(0, NX - 1), k], xs.at[c, k], xr.at[s, c, k]).wait_send()

    def sent_sum(s, c):
        rs_y(s, c).wait_send()
        for k in range(2):
            all_of(sz.at[s, c, k, pl.ds(1, NZ - 1)], bzs.at[c, k], bzr.at[s, c, k]).wait_send()
            all_of(gb.at[s, c, pl.ds(0, NX - 1), k], bxs.at[c, k], bxr.at[s, c, k, 0]).wait_send()

    both = range(STREAMS)

    def middle(s):
        for c in both:
            ag_pass(s, c, 0)
        for c in both:
            ag_turn(s, c)
        for c in both:
            ag_pass(s, c, 1)

    for c in both:
        ag_begin(0, c)
    loop(islands, lambda i: outer(i).start(), 1)
    loop(NZ, lambda d: count_z(d).start(), 1)
    for s in range(2):
        mask[s] = jnp.broadcast_to(retained[s], (128, 256)).T
    middle(0)

    all_small(0).wait_recv()
    cbuf[1] = cbuf[0] + jnp.sum(cz[1:], axis=0)
    loop(NX, lambda d: count_x(d).start(), 1)

    all_small(3).wait_recv()
    summed = dbuf[...] + jnp.sum(dz[1:], axis=0)
    outer_mean = jnp.broadcast_to((summed / islands)[None], (8, 8, 128)).reshape(64, 128)
    outer_rows = OUTER_MOMENTUM * ov_ref[...] + outer_mean
    global_rows = gw_ref[...] - OUTER_RATE * (OUTER_MOMENTUM * outer_rows + outer_mean)
    g_out[...] = jnp.where(mine, global_rows, gw_ref[...])
    o_out[...] = jnp.where(mine, outer_rows, ov_ref[...])
    for c in both:
        gf[c] = fold(global_rows, c)

    feats[0].wait()
    compute(0, 0)

    all_small(1).wait_recv()
    cbuf[2] = cbuf[1] + jnp.sum(cx[1:], axis=0)
    count_y().start()

    compute(0, 1)
    for c in both:
        for k in (1, 0):
            gather_terms(0, c, k)
    for c in both:
        far_sum(0, c)

    count_y().wait_recv()
    counts = cbuf[2] + cy[...]
    first_total = jnp.sum(jnp.where(row8 == 0, counts, 0.0))
    second_total = jnp.sum(jnp.where(row8 == 1, counts, 0.0))

    for c in both:
        sent_gather(0, c)
    for c in both:
        velocity = INNER_MOMENTUM * vf[c] + own_sum(0, c) / first_total
        weight = wf[c] - INNER_RATE * velocity
        weight = jnp.where(mine_folded, MERGE_WEIGHT * gf[c] + (1.0 - MERGE_WEIGHT) * weight, weight)
        wg[1, c, x, 0, 0] = weight.astype(bf16)
        ag_begin(1, c)
        vf[c] = velocity
        wf[c] = weight

    middle(1)
    for c in both:
        sent_sum(0, c)
    feats[1].wait()
    for c in both:
        compute(1, c)
    p_out[0] = jnp.where(lane < HALF, pred[0], turned(pred[1])).astype(bf16)
    for c in both:
        for k in (1, 0):
            gather_terms(1, c, k)
    for c in both:
        sent_gather(1, c)
    for j in (0, 1, 3):
        all_small(j).wait_send()
    count_y().wait_send()
    for c in both:
        far_sum(1, c)
    for c in both:
        velocity = INNER_MOMENTUM * vf[c] + own_sum(1, c) / second_total
        vf[c] = velocity
        wf[c] = wf[c] - INNER_RATE * velocity
    w_out[0] = unfold(wf[0], wf[1])
    v_out[0] = unfold(vf[0], vf[1])
    for c in both:
        sent_sum(1, c)


def write_out(*refs):
    ins, outs, held, (arrived, left) = refs[:5], refs[5:10], refs[10:15], refs[15:]
    loads = [pltpu.make_async_copy(a, b, arrived.at[i]) for i, (a, b) in enumerate(zip(ins, held))]
    stores = [pltpu.make_async_copy(a, b, left.at[i]) for i, (a, b) in enumerate(zip(held, outs))]
    for c in loads:
        c.start()
    for a, b in zip(loads, stores):
        a.wait()
        b.start()
    for c in stores:
        c.wait()


def local(
    features, targets, labels, fragment, local_weight, inner_velocity, global_weight, outer_velocity
):
    islands = lax.axis_size("island")
    f32, bf16 = jnp.float32, jnp.bfloat16
    vmem = pl.BlockSpec(memory_space=pltpu.VMEM)
    hbm = pl.BlockSpec(memory_space=pltpu.HBM)
    dma, V, C, G = pltpu.SemaphoreType.DMA, pltpu.VMEM, STREAMS, len(GROUPS)
    results = pl.pallas_call(
        functools.partial(kernel, islands),
        out_shape=(
            jax.ShapeDtypeStruct((1, 64, 128), f32),
            jax.ShapeDtypeStruct((1, 64, 128), f32),
            jax.ShapeDtypeStruct((64, 128), f32),
            jax.ShapeDtypeStruct((64, 128), f32),
            jax.ShapeDtypeStruct((1, 256, 128), bf16),
        ),
        in_specs=[
            pl.BlockSpec(memory_space=pltpu.SMEM), hbm, hbm, hbm, hbm, hbm, hbm, hbm,
        ],
        out_specs=(vmem,) * 5,
        scratch_shapes=[
            V((2, 1, 256, 128), bf16),
            V((2, 1, 256), jnp.int32),
            V((1, 64, 128), f32), V((1, 64, 128), f32),
            V((64, 128), f32), V((64, 128), f32),
            V((2, 256, 4096), bf16),
            V((2, C, NX, NY, NZ, 32, 128), bf16),
            V((NX, NZ * 64, 128), bf16),
            V((C, 2, NZ, 32, 128), f32),
            V((2, C, NX, NY, NZ, 32, 128), bf16),
            V((2, C, 2, NX, NZ, 32, 128), bf16),
            V((2, C, 2, NZ, 32, 128), bf16),
            V((2, C, 2, NZ, 32, 128), bf16),
            V((2, C, 32, 128), bf16),
            V((2, C, 32, 128), bf16),
            V((3, 8, 128), f32),
            V((NZ, 8, 128), f32),
            V((NX, 8, 128), f32),
            V((8, 128), f32),
            V((8, 128), f32),
            V((islands, 8, 128), f32),
            V((C, 2, 32, 128), f32),
            V((C, 32, 128), f32), V((C, 32, 128), f32), V((C, 32, 128), f32),
            V((2, 256, 128), f32), V((C, 256, 128), f32),
            dma((6,)), dma((2,)),
            dma((C, 2)), dma((2, C, 2, G)),
            dma((C, 2)), dma((2, C, 2)),
            dma((C,)), dma((2, C)),
            dma((C, 2)), dma((2, C, 2, G)),
            dma((C, 2)), dma((2, C, 2)),
            dma((C,)), dma((2, C)),
            dma((4,)), dma((4,)),
        ],
        compiler_params=pltpu.CompilerParams(
            collective_id=0, has_side_effects=True, vmem_limit_bytes=63 << 20
        ),
        cost_estimate=pl.CostEstimate(flops=1 << 30, bytes_accessed=5 << 20, transcendentals=0),
    )(fragment, features, targets, labels, local_weight, inner_velocity, global_weight, outer_velocity)
    return pl.pallas_call(
        write_out,
        out_shape=[jax.ShapeDtypeStruct(r.shape, r.dtype) for r in results],
        in_specs=[hbm] * 5,
        out_specs=[hbm] * 5,
        scratch_shapes=[V(r.shape, r.dtype) for r in results] + [dma((5,)), dma((5,))],
        compiler_params=pltpu.CompilerParams(vmem_limit_bytes=63 << 20),
    )(*results)


def solution(mesh):
    return jax.shard_map(
        local,
        mesh=mesh,
        in_specs=(
            P(None, "island", "fsdp", None),
            P(None, "island", "fsdp", None),
            P(None, "island", "fsdp"),
            P(),
            P("island", "fsdp", None),
            P("island", "fsdp", None),
            P("fsdp", None),
            P("fsdp", None),
        ),
        out_specs=(
            P("island", "fsdp", None),
            P("island", "fsdp", None),
            P("fsdp", None),
            P("fsdp", None),
            P("island", "fsdp", None),
        ),
        check_vma=False,
    )
```

```python
import functools

import jax
import jax.numpy as jnp
from jax import lax
from jax.experimental import pallas as pl
from jax.experimental.pallas import tpu as pltpu
from jax.sharding import PartitionSpec as P

FRAG = 16
FBLK = 4

INNER_RATE = 0.3
INNER_MOMENTUM = 0.9
OUTER_RATE = 0.7
OUTER_MOMENTUM = 0.9
MERGE_WEIGHT = 0.5

NX, NY, NZ = 4, 2, 8
MESH = pl.DeviceIdType.MESH


OFF = (0, 1, 7, 2, 6, 3, 5, 4)
GROUPS = ((0, 1), (1, 3), (3, 5), (5, 8))
NEAR = 2
STREAMS = 2
HALF = 64


def turned(a):
    return pltpu.roll(a, HALF, 1)


def kernel(
    islands,
    frag_ref, feat_hbm, tgt_hbm, lab_hbm, w_hbm, v_hbm, gw_hbm, ov_hbm,
    w_out, v_out, g_out, o_out, p_out,
    tgt_ref, lab_ref, w_ref, v_ref, gw_ref, ov_ref,
    xbuf, wg, piece, grad, gb, rx, sz, rz, sy, ry, cbuf, cz, cx, cy, dbuf, dz, keep,
    wf, vf, gf, mask, pred, err,
    load_sem, feat_sem, zs, zr, xs, xr, ys, yr, bxs, bxr, bzs, bzr, bys, byr,
    small_s, small_r,
):
    f32, bf16 = jnp.float32, jnp.bfloat16
    f = lax.axis_index("fsdp")
    isl = lax.axis_index("island")
    x, y, z = f // (NY * NZ), (f // NZ) % NY, f % NZ

    def dev(dx=0, dy=0, dz_=0):
        return {"fsdp": (((x + dx) % NX) * NY + (y + dy) % NY) * NZ + (z + dz_) % NZ}

    def peer(i):
        return {"island": (isl + i) % islands}

    def remote(src, dst, ss, rs, to):
        return pltpu.make_async_remote_copy(src, dst, ss, rs, device_id=to, device_id_type=MESH)

    def loop(n, body, start=0):
        def step(i, c):
            body(i)
            return c
        lax.fori_loop(start, n, step, 0)

    pairs = (
        (w_hbm, w_ref), (lab_hbm, lab_ref), (gw_hbm, gw_ref), (v_hbm, v_ref), (ov_hbm, ov_ref), (tgt_hbm, tgt_ref),
    )
    loads = [pltpu.make_async_copy(a, b, load_sem.at[i]) for i, (a, b) in enumerate(pairs)]
    feats = [pltpu.make_async_copy(feat_hbm.at[s, 0], xbuf.at[s], feat_sem.at[s]) for s in range(2)]

    barrier = pltpu.get_barrier_semaphore()

    def greet(to):
        pl.semaphore_signal(barrier, inc=1, device_id=to, device_id_type=MESH)

    loop(NZ, lambda d: greet(dev(dz_=d)), 1)
    loop(NX, lambda d: greet(dev(dx=d)), 1)
    greet(dev(dy=1))
    loop(islands, lambda i: greet(peer(i)), 1)
    for c in loads + feats:
        c.start()
    for c in loads:
        c.wait()

    lane32 = lax.broadcasted_iota(jnp.int32, (32, 128), 1)
    lane = lax.broadcasted_iota(jnp.int32, (256, 128), 1)

    def fold(a, c):
        low, high = a[:32], a[32:]
        if c == 0:
            return jnp.where(lane32 < HALF, low, turned(high))
        return jnp.where(lane32 < HALF, turned(low), high)

    def unfold(a, b):
        return jnp.concatenate([
            jnp.where(lane32 < HALF, a, turned(b)), jnp.where(lane32 < HALF, turned(a), b),
        ], axis=0)

    for c in range(STREAMS):
        wf[c] = fold(w_ref[0], c)
        wg[0, c, x, 0, 0] = wf[c].astype(bf16)
        vf[c] = fold(v_ref[0], c)
    retained = [(lab_ref[s] >= 0).astype(f32) for s in range(2)]
    halves = [r[:, :128] + r[:, 128:] for r in retained]
    row8 = lax.broadcasted_iota(jnp.int32, (8, 128), 0)
    cbuf[0] = jnp.where(row8 == 0, halves[0], jnp.where(row8 == 1, halves[1], 0.0))
    chosen = frag_ref[0] & (FRAG - 1)
    rows = lax.broadcasted_iota(jnp.int32, (64, 128), 0)
    mine = (rows // FBLK) == chosen
    rows32 = lax.broadcasted_iota(jnp.int32, (32, 128), 0) + jnp.where(lane32 < HALF, 0, 32)
    mine_folded = (rows32 // FBLK) == chosen
    diff = jnp.where(mine, gw_ref[...] - w_ref[0], 0.0)
    dbuf[...] = jnp.sum(diff.reshape(8, 8, 128), axis=0)

    pl.semaphore_wait(barrier, (NZ - 1) + (NX - 1) + 1 + (islands - 1))

    def which(k):
        return (y + k) % NY

    def ag_y(s, c):
        return remote(wg.at[s, c, x, 0, 0], wg.at[s, c, x, 1, 0], ys.at[c], yr.at[s, c], dev(dy=1))

    def ag_z(s, c, k, i):
        g = [lo <= i < hi for lo, hi in GROUPS].index(True)
        return remote(
            wg.at[s, c, x, k, 0], wg.at[s, c, x, k, i], zs.at[c, k], zr.at[s, c, k, g], dev(dz_=NZ - OFF[i])
        )

    def ag_x(s, c, k, g, dx):
        blk = wg.at[s, c, x, k, pl.ds(GROUPS[g][0], GROUPS[g][1] - GROUPS[g][0])]
        return remote(blk, blk, xs.at[c, k], xr.at[s, c, k], dev(dx=dx))

    def all_of(ref, ss, rs):
        return remote(ref, ref, ss, rs, dev(dx=1))

    def ag_open(s, c, k):
        for i in range(1, NZ):
            ag_z(s, c, k, i).start()

    def ag_pass(s, c, k, groups=range(len(GROUPS))):
        for g in groups:
            lo, hi = GROUPS[g]
            first = max(lo, 1)
            if first < hi:
                all_of(wg.at[s, c, x, k, pl.ds(first, hi - first)], zs.at[c, k], zr.at[s, c, k, g]).wait_recv()
            for dx in (2, 1, 3):
                ag_x(s, c, k, g, dx).start()

    def ag_wait(s, c, k):
        all_of(wg.at[s, c, pl.ds(0, NX - 1), k], xs.at[c, k], xr.at[s, c, k]).wait_recv()

    def ag_begin(s, c):
        ag_y(s, c).start()
        ag_open(s, c, 0)

    def ag_turn(s, c):
        ag_y(s, c).wait_recv()
        ag_open(s, c, 1)

    def count_z(d):
        return remote(cbuf.at[0], cz.at[d], small_s.at[0], small_r.at[0], dev(dz_=d))

    def count_x(d):
        return remote(cbuf.at[1], cx.at[d], small_s.at[1], small_r.at[1], dev(dx=d))

    def count_y():
        return remote(cbuf.at[2], cy, small_s.at[2], small_r.at[2], dev(dy=1))

    def outer(i):
        return remote(dbuf, dz.at[i], small_s.at[3], small_r.at[3], peer(i))

    def all_small(j):
        ref, n = ((cz, NZ), (cx, NX), None, (dz, islands))[j]
        return all_of(ref.at[pl.ds(1, n - 1)], small_s.at[j], small_r.at[j])

    def rs_x(s, c, k, g, dx):
        part = pl.ds(GROUPS[g][0], GROUPS[g][1] - GROUPS[g][0])
        return remote(
            gb.at[s, c, (x + dx) % NX, k, part], rx.at[s, c, k, dx, part],
            bxs.at[c, k], bxr.at[s, c, k, g], dev(dx=dx),
        )

    def rs_z(s, c, k, i):
        return remote(sz.at[s, c, k, i], rz.at[s, c, k, i], bzs.at[c, k], bzr.at[s, c, k], dev(dz_=OFF[i]))

    def rs_y(s, c):
        return remote(sy.at[s, c], ry.at[s, c], bys.at[c], byr.at[s, c], dev(dy=1))

    def columns(xx, yy):
        return pl.ds(pl.multiple_of((xx * NY + yy) * (NZ * 64), NZ * 64), NZ * 64)

    def forward(s, c, k, acc):
        def body(xx, acc):
            for i in range(NZ):
                at = pl.multiple_of(((z + OFF[i]) % NZ) * 64, 64)
                block = wg[s, c, xx, k, i]
                piece[xx, pl.ds(at, 32)] = block
                piece[xx, pl.ds(at + 32, 32)] = turned(block.astype(f32)).astype(bf16)
            return acc + jnp.dot(xbuf[s, :, columns(xx, which(k))], piece[xx], preferred_element_type=f32)
        return lax.fori_loop(0, NX, body, acc)

    def terms(s, c, k, dx):
        xx = (x + dx) % NX
        part = lax.dot_general(
            xbuf[s, :, columns(xx, which(k))], err[c], (((0,), (0,)), ((), ())), preferred_element_type=f32
        ).reshape(NZ, 2, 32, 128)
        low, high = part[:, 0].reshape(NZ * 32, 128), part[:, 1].reshape(NZ * 32, 128)
        folded = (low + turned(high)).reshape(NZ, 32, 128)
        for zz in range(NZ):
            e = (zz - z + NZ) % NZ
            slot = jnp.where(e == 0, 0, jnp.where(e <= NZ // 2, 2 * e - 1, 2 * (NZ - e)))
            yield xx, slot, folded[zz]

    def spread(s, c, k):
        for dx in (2, 1, 3):
            for xx, slot, part in terms(s, c, k, dx):
                gb[s, c, xx, k, slot] = part.astype(bf16)
            for g in reversed(range(len(GROUPS))):
                rs_x(s, c, k, g, dx).start()

    def own_terms(s, c, k):
        for _, slot, part in terms(s, c, k, 0):
            grad[c, k, slot] = part

    def gather_terms(s, c, k):
        for g in reversed(range(len(GROUPS))):
            lo, hi = GROUPS[g]
            part = rx.at[s, c, k, pl.ds(1, NX - 1), pl.ds(lo, hi - lo)]
            all_of(part, bxs.at[c, k], bxr.at[s, c, k, g]).wait_recv()
            t = grad[c, k, lo:hi]
            for dx in (1, 2, 3):
                t = t + rx[s, c, k, dx, lo:hi].astype(f32)
            sz[s, c, k, lo:hi] = t.astype(bf16)
            if lo == 0:
                keep[c, k] = t[0]
            for i in range(hi - 1, max(lo, 1) - 1, -1):
                rs_z(s, c, k, i).start()

    def plane(s, c, k):
        t = keep[c, k]
        all_of(rz.at[s, c, k, pl.ds(1, NZ - 1)], bzs.at[c, k], bzr.at[s, c, k]).wait_recv()
        for i in range(1, NZ):
            t = t + rz[s, c, k, i].astype(f32)
        return t

    def far_sum(s, c):
        sy[s, c] = plane(s, c, 1).astype(bf16)
        rs_y(s, c).start()

    def own_sum(s, c):
        t = plane(s, c, 0)
        rs_y(s, c).wait_recv()
        return t + ry[s, c].astype(f32)

    def errors_of(s, c, predicted):
        target = tgt_ref[s, 0].astype(f32)
        if c:
            target = turned(target)
        return jnp.where(lane < HALF, mask[s] * (predicted - target), 0.0).astype(bf16)

    def compute(s, c):
        acc = jnp.zeros((256, 128), f32)
        for k in range(2):
            ag_wait(s, c, k)
            acc = forward(s, c, k, acc)
        if s == 1:
            pred[c] = acc
        err[c] = errors_of(s, c, acc)
        spread(s, c, 1)

    def sent_gather(s, c):
        ag_y(s, c).wait_send()
        for k in range(2):
            all_of(wg.at[s, c, x, k, pl.ds(1, NZ - 1)], zs.at[c, k], zr.at[s, c, k, 0]).wait_send()
            all_of(wg.at[s, c, pl.ds(0, NX - 1), k], xs.at[c, k], xr.at[s, c, k]).wait_send()

    def sent_sum(s, c):
        rs_y(s, c).wait_send()
        for k in range(2):
            all_of(sz.at[s, c, k, pl.ds(1, NZ - 1)], bzs.at[c, k], bzr.at[s, c, k]).wait_send()
            all_of(gb.at[s, c, pl.ds(0, NX - 1), k], bxs.at[c, k], bxr.at[s, c, k, 0]).wait_send()

    both = range(STREAMS)

    def middle(s):
        for c in both:
            ag_pass(s, c, 0, range(NEAR))
        for c in both:
            ag_turn(s, c)
        for c in both:
            ag_pass(s, c, 0, range(NEAR, len(GROUPS)))
        for c in both:
            ag_pass(s, c, 1)

    for c in both:
        ag_y(0, c).start()
    for c in both:
        ag_open(0, c, 0)
    loop(islands, lambda i: outer(i).start(), 1)
    loop(NZ, lambda d: count_z(d).start(), 1)
    for s in range(2):
        mask[s] = jnp.broadcast_to(retained[s], (128, 256)).T
    middle(0)

    all_small(0).wait_recv()
    cbuf[1] = cbuf[0] + jnp.sum(cz[1:], axis=0)
    loop(NX, lambda d: count_x(d).start(), 1)

    all_small(3).wait_recv()
    summed = dbuf[...] + jnp.sum(dz[1:], axis=0)
    outer_mean = jnp.broadcast_to((summed / islands)[None], (8, 8, 128)).reshape(64, 128)
    outer_rows = OUTER_MOMENTUM * ov_ref[...] + outer_mean
    global_rows = gw_ref[...] - OUTER_RATE * (OUTER_MOMENTUM * outer_rows + outer_mean)
    g_out[...] = jnp.where(mine, global_rows, gw_ref[...])
    o_out[...] = jnp.where(mine, outer_rows, ov_ref[...])
    for c in both:
        gf[c] = fold(global_rows, c)

    feats[0].wait()
    compute(0, 0)

    all_small(1).wait_recv()
    cbuf[2] = cbuf[1] + jnp.sum(cx[1:], axis=0)
    count_y().start()

    compute(0, 1)
    for c in both:
        spread(0, c, 0)
    for k in (1, 0):
        for c in both:
            own_terms(0, c, k)
    for k in (1, 0):
        for c in both:
            gather_terms(0, c, k)
    for c in both:
        far_sum(0, c)

    count_y().wait_recv()
    counts = cbuf[2] + cy[...]
    first_total = jnp.sum(jnp.where(row8 == 0, counts, 0.0))
    second_total = jnp.sum(jnp.where(row8 == 1, counts, 0.0))

    for c in both:
        sent_gather(0, c)
    for c in both:
        velocity = INNER_MOMENTUM * vf[c] + own_sum(0, c) / first_total
        weight = wf[c] - INNER_RATE * velocity
        weight = jnp.where(mine_folded, MERGE_WEIGHT * gf[c] + (1.0 - MERGE_WEIGHT) * weight, weight)
        wg[1, c, x, 0, 0] = weight.astype(bf16)
        ag_begin(1, c)
        vf[c] = velocity
        wf[c] = weight

    middle(1)
    for c in both:
        sent_sum(0, c)
    feats[1].wait()
    for c in both:
        compute(1, c)
    p_out[0] = jnp.where(lane < HALF, pred[0], turned(pred[1])).astype(bf16)
    for c in both:
        spread(1, c, 0)
    for k in (1, 0):
        for c in both:
            own_terms(1, c, k)
    for k in (1, 0):
        for c in both:
            gather_terms(1, c, k)
    for c in both:
        sent_gather(1, c)
    for j in (0, 1, 3):
        all_small(j).wait_send()
    count_y().wait_send()
    for c in both:
        far_sum(1, c)
    for c in both:
        velocity = INNER_MOMENTUM * vf[c] + own_sum(1, c) / second_total
        vf[c] = velocity
        wf[c] = wf[c] - INNER_RATE * velocity
    w_out[0] = unfold(wf[0], wf[1])
    v_out[0] = unfold(vf[0], vf[1])
    for c in both:
        sent_sum(1, c)


def write_out(*refs):
    ins, outs, held, (arrived, left) = refs[:5], refs[5:10], refs[10:15], refs[15:]
    loads = [pltpu.make_async_copy(a, b, arrived.at[i]) for i, (a, b) in enumerate(zip(ins, held))]
    stores = [pltpu.make_async_copy(a, b, left.at[i]) for i, (a, b) in enumerate(zip(held, outs))]
    for c in loads:
        c.start()
    for a, b in zip(loads, stores):
        a.wait()
        b.start()
    for c in stores:
        c.wait()


def local(
    features, targets, labels, fragment, local_weight, inner_velocity, global_weight, outer_velocity
):
    islands = lax.axis_size("island")
    f32, bf16 = jnp.float32, jnp.bfloat16
    vmem = pl.BlockSpec(memory_space=pltpu.VMEM)
    hbm = pl.BlockSpec(memory_space=pltpu.HBM)
    dma, V, C, G = pltpu.SemaphoreType.DMA, pltpu.VMEM, STREAMS, len(GROUPS)
    results = pl.pallas_call(
        functools.partial(kernel, islands),
        out_shape=(
            jax.ShapeDtypeStruct((1, 64, 128), f32),
            jax.ShapeDtypeStruct((1, 64, 128), f32),
            jax.ShapeDtypeStruct((64, 128), f32),
            jax.ShapeDtypeStruct((64, 128), f32),
            jax.ShapeDtypeStruct((1, 256, 128), bf16),
        ),
        in_specs=[
            pl.BlockSpec(memory_space=pltpu.SMEM), hbm, hbm, hbm, hbm, hbm, hbm, hbm,
        ],
        out_specs=(vmem,) * 5,
        scratch_shapes=[
            V((2, 1, 256, 128), bf16),
            V((2, 1, 256), jnp.int32),
            V((1, 64, 128), f32), V((1, 64, 128), f32),
            V((64, 128), f32), V((64, 128), f32),
            V((2, 256, 4096), bf16),
            V((2, C, NX, NY, NZ, 32, 128), bf16),
            V((NX, NZ * 64, 128), bf16),
            V((C, 2, NZ, 32, 128), f32),
            V((2, C, NX, NY, NZ, 32, 128), bf16),
            V((2, C, 2, NX, NZ, 32, 128), bf16),
            V((2, C, 2, NZ, 32, 128), bf16),
            V((2, C, 2, NZ, 32, 128), bf16),
            V((2, C, 32, 128), bf16),
            V((2, C, 32, 128), bf16),
            V((3, 8, 128), f32),
            V((NZ, 8, 128), f32),
            V((NX, 8, 128), f32),
            V((8, 128), f32),
            V((8, 128), f32),
            V((islands, 8, 128), f32),
            V((C, 2, 32, 128), f32),
            V((C, 32, 128), f32), V((C, 32, 128), f32), V((C, 32, 128), f32),
            V((2, 256, 128), f32), V((C, 256, 128), f32),
            V((C, 256, 128), bf16),
            dma((6,)), dma((2,)),
            dma((C, 2)), dma((2, C, 2, G)),
            dma((C, 2)), dma((2, C, 2)),
            dma((C,)), dma((2, C)),
            dma((C, 2)), dma((2, C, 2, G)),
            dma((C, 2)), dma((2, C, 2)),
            dma((C,)), dma((2, C)),
            dma((4,)), dma((4,)),
        ],
        compiler_params=pltpu.CompilerParams(
            collective_id=0, has_side_effects=True, vmem_limit_bytes=63 << 20
        ),
        cost_estimate=pl.CostEstimate(flops=1 << 30, bytes_accessed=5 << 20, transcendentals=0),
    )(fragment, features, targets, labels, local_weight, inner_velocity, global_weight, outer_velocity)
    return pl.pallas_call(
        write_out,
        out_shape=[jax.ShapeDtypeStruct(r.shape, r.dtype) for r in results],
        in_specs=[hbm] * 5,
        out_specs=[hbm] * 5,
        scratch_shapes=[V(r.shape, r.dtype) for r in results] + [dma((5,)), dma((5,))],
        compiler_params=pltpu.CompilerParams(vmem_limit_bytes=63 << 20),
    )(*results)


def solution(mesh):
    return jax.shard_map(
        local,
        mesh=mesh,
        in_specs=(
            P(None, "island", "fsdp", None),
            P(None, "island", "fsdp", None),
            P(None, "island", "fsdp"),
            P(),
            P("island", "fsdp", None),
            P("island", "fsdp", None),
            P("fsdp", None),
            P("fsdp", None),
        ),
        out_specs=(
            P("island", "fsdp", None),
            P("island", "fsdp", None),
            P("fsdp", None),
            P("fsdp", None),
            P("island", "fsdp", None),
        ),
        check_vma=False,
    )
```

```python
import functools

import jax
import jax.numpy as jnp
from jax import lax
from jax.experimental import pallas as pl
from jax.experimental.pallas import tpu as pltpu
from jax.sharding import PartitionSpec as P

FRAG = 16
FBLK = 4

INNER_RATE = 0.3
INNER_MOMENTUM = 0.9
OUTER_RATE = 0.7
OUTER_MOMENTUM = 0.9
MERGE_WEIGHT = 0.5

NX, NY, NZ = 4, 2, 8
MESH = pl.DeviceIdType.MESH


OFF = (0, 1, 7, 2, 6, 3, 5, 4)
GROUPS = ((0, 1), (1, 3), (3, 5), (5, 7), (7, 8))
NEAR = 2
STREAMS = 2
HALF = 64


def turned(a):
    return pltpu.roll(a, HALF, 1)


def kernel(
    islands,
    frag_ref, feat_hbm, tgt_hbm, lab_hbm, w_hbm, v_hbm, gw_hbm, ov_hbm,
    w_out, v_out, g_out, o_out, p_out,
    tgt_ref, lab_ref, w_ref, v_ref, gw_ref, ov_ref,
    xbuf, wg, piece, grad, gb, rx, sz, rz, sy, ry, cbuf, cz, cx, cy, dbuf, dz, keep,
    wf, vf, gf, mask, pred, err,
    load_sem, feat_sem, zs, zr, xs, xr, ys, yr, bxs, bxr, bzs, bzr, bys, byr,
    small_s, small_r,
):
    f32, bf16 = jnp.float32, jnp.bfloat16
    f = lax.axis_index("fsdp")
    isl = lax.axis_index("island")
    x, y, z = f // (NY * NZ), (f // NZ) % NY, f % NZ

    def dev(dx=0, dy=0, dz_=0):
        return {"fsdp": (((x + dx) % NX) * NY + (y + dy) % NY) * NZ + (z + dz_) % NZ}

    def peer(i):
        return {"island": (isl + i) % islands}

    def remote(src, dst, ss, rs, to):
        return pltpu.make_async_remote_copy(src, dst, ss, rs, device_id=to, device_id_type=MESH)

    def loop(n, body, start=0):
        def step(i, c):
            body(i)
            return c
        lax.fori_loop(start, n, step, 0)

    pairs = (
        (w_hbm, w_ref), (lab_hbm, lab_ref), (gw_hbm, gw_ref), (v_hbm, v_ref), (ov_hbm, ov_ref), (tgt_hbm, tgt_ref),
    )
    loads = [pltpu.make_async_copy(a, b, load_sem.at[i]) for i, (a, b) in enumerate(pairs)]
    feats = [pltpu.make_async_copy(feat_hbm.at[s, 0], xbuf.at[s], feat_sem.at[s]) for s in range(2)]

    barrier = pltpu.get_barrier_semaphore()

    def greet(to):
        pl.semaphore_signal(barrier, inc=1, device_id=to, device_id_type=MESH)

    loop(NZ, lambda d: greet(dev(dz_=d)), 1)
    loop(NX, lambda d: greet(dev(dx=d)), 1)
    greet(dev(dy=1))
    loop(islands, lambda i: greet(peer(i)), 1)
    for c in loads + feats:
        c.start()
    for c in loads:
        c.wait()

    lane32 = lax.broadcasted_iota(jnp.int32, (32, 128), 1)
    lane = lax.broadcasted_iota(jnp.int32, (256, 128), 1)

    def fold(a, c):
        low, high = a[:32], a[32:]
        if c == 0:
            return jnp.where(lane32 < HALF, low, turned(high))
        return jnp.where(lane32 < HALF, turned(low), high)

    def unfold(a, b):
        return jnp.concatenate([
            jnp.where(lane32 < HALF, a, turned(b)), jnp.where(lane32 < HALF, turned(a), b),
        ], axis=0)

    for c in range(STREAMS):
        wf[c] = fold(w_ref[0], c)
        wg[0, c, x, 0, 0] = wf[c].astype(bf16)
        vf[c] = fold(v_ref[0], c)
    retained = [(lab_ref[s] >= 0).astype(f32) for s in range(2)]
    halves = [r[:, :128] + r[:, 128:] for r in retained]
    row8 = lax.broadcasted_iota(jnp.int32, (8, 128), 0)
    cbuf[0] = jnp.where(row8 == 0, halves[0], jnp.where(row8 == 1, halves[1], 0.0))
    chosen = frag_ref[0] & (FRAG - 1)
    rows = lax.broadcasted_iota(jnp.int32, (64, 128), 0)
    mine = (rows // FBLK) == chosen
    rows32 = lax.broadcasted_iota(jnp.int32, (32, 128), 0) + jnp.where(lane32 < HALF, 0, 32)
    mine_folded = (rows32 // FBLK) == chosen
    diff = jnp.where(mine, gw_ref[...] - w_ref[0], 0.0)
    dbuf[...] = jnp.sum(diff.reshape(8, 8, 128), axis=0)

    pl.semaphore_wait(barrier, (NZ - 1) + (NX - 1) + 1 + (islands - 1))

    def which(k):
        return (y + k) % NY

    def ag_y(s, c):
        return remote(wg.at[s, c, x, 0, 0], wg.at[s, c, x, 1, 0], ys.at[c], yr.at[s, c], dev(dy=1))

    def ag_z(s, c, k, i):
        g = [lo <= i < hi for lo, hi in GROUPS].index(True)
        return remote(
            wg.at[s, c, x, k, 0], wg.at[s, c, x, k, i], zs.at[c, k], zr.at[s, c, k, g], dev(dz_=NZ - OFF[i])
        )

    def ag_x(s, c, k, g, dx):
        blk = wg.at[s, c, x, k, pl.ds(GROUPS[g][0], GROUPS[g][1] - GROUPS[g][0])]
        return remote(blk, blk, xs.at[c, k], xr.at[s, c, k], dev(dx=dx))

    def all_of(ref, ss, rs):
        return remote(ref, ref, ss, rs, dev(dx=1))

    def ag_open(s, c, k):
        for i in range(1, NZ):
            ag_z(s, c, k, i).start()

    def ag_pass(s, c, k, groups=range(len(GROUPS))):
        for g in groups:
            lo, hi = GROUPS[g]
            first = max(lo, 1)
            if first < hi:
                all_of(wg.at[s, c, x, k, pl.ds(first, hi - first)], zs.at[c, k], zr.at[s, c, k, g]).wait_recv()
            for dx in (2, 1, 3):
                ag_x(s, c, k, g, dx).start()

    def ag_wait(s, c, k):
        all_of(wg.at[s, c, pl.ds(0, NX - 1), k], xs.at[c, k], xr.at[s, c, k]).wait_recv()

    def ag_begin(s, c):
        ag_y(s, c).start()
        ag_open(s, c, 0)

    def ag_turn(s, c):
        ag_y(s, c).wait_recv()
        ag_open(s, c, 1)

    def count_z(d):
        return remote(cbuf.at[0], cz.at[d], small_s.at[0], small_r.at[0], dev(dz_=d))

    def count_x(d):
        return remote(cbuf.at[1], cx.at[d], small_s.at[1], small_r.at[1], dev(dx=d))

    def count_y():
        return remote(cbuf.at[2], cy, small_s.at[2], small_r.at[2], dev(dy=1))

    def outer(i):
        return remote(dbuf, dz.at[i], small_s.at[3], small_r.at[3], peer(i))

    def all_small(j):
        ref, n = ((cz, NZ), (cx, NX), None, (dz, islands))[j]
        return all_of(ref.at[pl.ds(1, n - 1)], small_s.at[j], small_r.at[j])

    def rs_x(s, c, k, g, dx):
        part = pl.ds(GROUPS[g][0], GROUPS[g][1] - GROUPS[g][0])
        return remote(
            gb.at[s, c, (x + dx) % NX, k, part], rx.at[s, c, k, dx, part],
            bxs.at[c, k], bxr.at[s, c, k, g], dev(dx=dx),
        )

    def rs_z(s, c, k, i):
        return remote(sz.at[s, c, k, i], rz.at[s, c, k, i], bzs.at[c, k], bzr.at[s, c, k], dev(dz_=OFF[i]))

    def rs_y(s, c):
        return remote(sy.at[s, c], ry.at[s, c], bys.at[c], byr.at[s, c], dev(dy=1))

    def columns(xx, yy):
        return pl.ds(pl.multiple_of((xx * NY + yy) * (NZ * 64), NZ * 64), NZ * 64)

    def forward(s, c, k, acc):
        def body(xx, acc):
            for i in range(NZ):
                at = pl.multiple_of(((z + OFF[i]) % NZ) * 64, 64)
                block = wg[s, c, xx, k, i]
                piece[xx, pl.ds(at, 32)] = block
                piece[xx, pl.ds(at + 32, 32)] = turned(block.astype(f32)).astype(bf16)
            return acc + jnp.dot(xbuf[s, :, columns(xx, which(k))], piece[xx], preferred_element_type=f32)
        return lax.fori_loop(0, NX, body, acc)

    def terms(s, c, k, dx):
        xx = (x + dx) % NX
        part = lax.dot_general(
            xbuf[s, :, columns(xx, which(k))], err[c], (((0,), (0,)), ((), ())), preferred_element_type=f32
        ).reshape(NZ, 2, 32, 128)
        low, high = part[:, 0].reshape(NZ * 32, 128), part[:, 1].reshape(NZ * 32, 128)
        folded = (low + turned(high)).reshape(NZ, 32, 128)
        for zz in range(NZ):
            e = (zz - z + NZ) % NZ
            slot = jnp.where(e == 0, 0, jnp.where(e <= NZ // 2, 2 * e - 1, 2 * (NZ - e)))
            yield xx, slot, folded[zz]

    def spread(s, c, k):
        for dx in (2, 1, 3):
            for xx, slot, part in terms(s, c, k, dx):
                gb[s, c, xx, k, slot] = part.astype(bf16)
            for g in reversed(range(len(GROUPS))):
                rs_x(s, c, k, g, dx).start()

    def own_terms(s, c, k):
        for _, slot, part in terms(s, c, k, 0):
            grad[c, k, slot] = part

    def gather_terms(s, c, k):
        for g in reversed(range(len(GROUPS))):
            lo, hi = GROUPS[g]
            part = rx.at[s, c, k, pl.ds(1, NX - 1), pl.ds(lo, hi - lo)]
            all_of(part, bxs.at[c, k], bxr.at[s, c, k, g]).wait_recv()
            t = grad[c, k, lo:hi]
            for dx in (1, 2, 3):
                t = t + rx[s, c, k, dx, lo:hi].astype(f32)
            sz[s, c, k, lo:hi] = t.astype(bf16)
            if lo == 0:
                keep[c, k] = t[0]
            for i in range(hi - 1, max(lo, 1) - 1, -1):
                rs_z(s, c, k, i).start()

    def plane(s, c, k):
        t = keep[c, k]
        all_of(rz.at[s, c, k, pl.ds(1, NZ - 1)], bzs.at[c, k], bzr.at[s, c, k]).wait_recv()
        for i in range(1, NZ):
            t = t + rz[s, c, k, i].astype(f32)
        return t

    def far_sum(s, c):
        sy[s, c] = plane(s, c, 1).astype(bf16)
        rs_y(s, c).start()

    def own_sum(s, c):
        t = plane(s, c, 0)
        rs_y(s, c).wait_recv()
        return t + ry[s, c].astype(f32)

    def errors_of(s, c, predicted):
        target = tgt_ref[s, 0].astype(f32)
        if c:
            target = turned(target)
        return jnp.where(lane < HALF, mask[s] * (predicted - target), 0.0).astype(bf16)

    def compute(s, c):
        acc = jnp.zeros((256, 128), f32)
        for k in range(2):
            ag_wait(s, c, k)
            acc = forward(s, c, k, acc)
        if s == 1:
            pred[c] = acc
        err[c] = errors_of(s, c, acc)
        spread(s, c, 1)

    def sent_gather(s, c):
        ag_y(s, c).wait_send()
        for k in range(2):
            all_of(wg.at[s, c, x, k, pl.ds(1, NZ - 1)], zs.at[c, k], zr.at[s, c, k, 0]).wait_send()
            all_of(wg.at[s, c, pl.ds(0, NX - 1), k], xs.at[c, k], xr.at[s, c, k]).wait_send()

    def sent_sum(s, c):
        rs_y(s, c).wait_send()
        for k in range(2):
            all_of(sz.at[s, c, k, pl.ds(1, NZ - 1)], bzs.at[c, k], bzr.at[s, c, k]).wait_send()
            all_of(gb.at[s, c, pl.ds(0, NX - 1), k], bxs.at[c, k], bxr.at[s, c, k, 0]).wait_send()

    both = range(STREAMS)

    def middle(s):
        for c in both:
            ag_pass(s, c, 0, range(NEAR))
        for c in both:
            ag_turn(s, c)
        for c in both:
            ag_pass(s, c, 0, range(NEAR, len(GROUPS)))
        for c in both:
            ag_pass(s, c, 1)

    for c in both:
        ag_y(0, c).start()
    for c in both:
        ag_open(0, c, 0)
    loop(islands, lambda i: outer(i).start(), 1)
    loop(NZ, lambda d: count_z(d).start(), 1)
    for s in range(2):
        mask[s] = jnp.broadcast_to(retained[s], (128, 256)).T
    middle(0)

    all_small(0).wait_recv()
    cbuf[1] = cbuf[0] + jnp.sum(cz[1:], axis=0)
    loop(NX, lambda d: count_x(d).start(), 1)

    all_small(3).wait_recv()
    summed = dbuf[...] + jnp.sum(dz[1:], axis=0)
    outer_mean = jnp.broadcast_to((summed / islands)[None], (8, 8, 128)).reshape(64, 128)
    outer_rows = OUTER_MOMENTUM * ov_ref[...] + outer_mean
    global_rows = gw_ref[...] - OUTER_RATE * (OUTER_MOMENTUM * outer_rows + outer_mean)
    g_out[...] = jnp.where(mine, global_rows, gw_ref[...])
    o_out[...] = jnp.where(mine, outer_rows, ov_ref[...])
    for c in both:
        gf[c] = fold(global_rows, c)

    feats[0].wait()
    compute(0, 0)

    all_small(1).wait_recv()
    cbuf[2] = cbuf[1] + jnp.sum(cx[1:], axis=0)
    count_y().start()

    compute(0, 1)
    for c in both:
        spread(0, c, 0)
    for k in (1, 0):
        for c in both:
            own_terms(0, c, k)
    for k in (1, 0):
        for c in both:
            gather_terms(0, c, k)
    for c in both:
        far_sum(0, c)

    count_y().wait_recv()
    counts = cbuf[2] + cy[...]
    first_total = jnp.sum(jnp.where(row8 == 0, counts, 0.0))
    second_total = jnp.sum(jnp.where(row8 == 1, counts, 0.0))

    for c in both:
        sent_gather(0, c)
    for c in both:
        velocity = INNER_MOMENTUM * vf[c] + own_sum(0, c) / first_total
        weight = wf[c] - INNER_RATE * velocity
        weight = jnp.where(mine_folded, MERGE_WEIGHT * gf[c] + (1.0 - MERGE_WEIGHT) * weight, weight)
        wg[1, c, x, 0, 0] = weight.astype(bf16)
        ag_begin(1, c)
        vf[c] = velocity
        wf[c] = weight

    middle(1)
    for c in both:
        sent_sum(0, c)
    feats[1].wait()
    for c in both:
        compute(1, c)
    p_out[0] = jnp.where(lane < HALF, pred[0], turned(pred[1])).astype(bf16)
    for c in both:
        spread(1, c, 0)
    for k in (1, 0):
        for c in both:
            own_terms(1, c, k)
    for k in (1, 0):
        for c in both:
            gather_terms(1, c, k)
    for c in both:
        sent_gather(1, c)
    for j in (0, 1, 3):
        all_small(j).wait_send()
    count_y().wait_send()
    for c in both:
        far_sum(1, c)
    for c in both:
        velocity = INNER_MOMENTUM * vf[c] + own_sum(1, c) / second_total
        vf[c] = velocity
        wf[c] = wf[c] - INNER_RATE * velocity
    w_out[0] = unfold(wf[0], wf[1])
    v_out[0] = unfold(vf[0], vf[1])
    for c in both:
        sent_sum(1, c)


def write_out(*refs):
    ins, outs, held, (arrived, left) = refs[:5], refs[5:10], refs[10:15], refs[15:]
    loads = [pltpu.make_async_copy(a, b, arrived.at[i]) for i, (a, b) in enumerate(zip(ins, held))]
    stores = [pltpu.make_async_copy(a, b, left.at[i]) for i, (a, b) in enumerate(zip(held, outs))]
    for c in loads:
        c.start()
    for a, b in zip(loads, stores):
        a.wait()
        b.start()
    for c in stores:
        c.wait()


def local(
    features, targets, labels, fragment, local_weight, inner_velocity, global_weight, outer_velocity
):
    islands = lax.axis_size("island")
    f32, bf16 = jnp.float32, jnp.bfloat16
    vmem = pl.BlockSpec(memory_space=pltpu.VMEM)
    hbm = pl.BlockSpec(memory_space=pltpu.HBM)
    dma, V, C, G = pltpu.SemaphoreType.DMA, pltpu.VMEM, STREAMS, len(GROUPS)
    results = pl.pallas_call(
        functools.partial(kernel, islands),
        out_shape=(
            jax.ShapeDtypeStruct((1, 64, 128), f32),
            jax.ShapeDtypeStruct((1, 64, 128), f32),
            jax.ShapeDtypeStruct((64, 128), f32),
            jax.ShapeDtypeStruct((64, 128), f32),
            jax.ShapeDtypeStruct((1, 256, 128), bf16),
        ),
        in_specs=[
            pl.BlockSpec(memory_space=pltpu.SMEM), hbm, hbm, hbm, hbm, hbm, hbm, hbm,
        ],
        out_specs=(vmem,) * 5,
        scratch_shapes=[
            V((2, 1, 256, 128), bf16),
            V((2, 1, 256), jnp.int32),
            V((1, 64, 128), f32), V((1, 64, 128), f32),
            V((64, 128), f32), V((64, 128), f32),
            V((2, 256, 4096), bf16),
            V((2, C, NX, NY, NZ, 32, 128), bf16),
            V((NX, NZ * 64, 128), bf16),
            V((C, 2, NZ, 32, 128), f32),
            V((2, C, NX, NY, NZ, 32, 128), bf16),
            V((2, C, 2, NX, NZ, 32, 128), bf16),
            V((2, C, 2, NZ, 32, 128), bf16),
            V((2, C, 2, NZ, 32, 128), bf16),
            V((2, C, 32, 128), bf16),
            V((2, C, 32, 128), bf16),
            V((3, 8, 128), f32),
            V((NZ, 8, 128), f32),
            V((NX, 8, 128), f32),
            V((8, 128), f32),
            V((8, 128), f32),
            V((islands, 8, 128), f32),
            V((C, 2, 32, 128), f32),
            V((C, 32, 128), f32), V((C, 32, 128), f32), V((C, 32, 128), f32),
            V((2, 256, 128), f32), V((C, 256, 128), f32),
            V((C, 256, 128), bf16),
            dma((6,)), dma((2,)),
            dma((C, 2)), dma((2, C, 2, G)),
            dma((C, 2)), dma((2, C, 2)),
            dma((C,)), dma((2, C)),
            dma((C, 2)), dma((2, C, 2, G)),
            dma((C, 2)), dma((2, C, 2)),
            dma((C,)), dma((2, C)),
            dma((4,)), dma((4,)),
        ],
        compiler_params=pltpu.CompilerParams(
            collective_id=0, has_side_effects=True, vmem_limit_bytes=63 << 20
        ),
        cost_estimate=pl.CostEstimate(flops=1 << 30, bytes_accessed=5 << 20, transcendentals=0),
    )(fragment, features, targets, labels, local_weight, inner_velocity, global_weight, outer_velocity)
    return pl.pallas_call(
        write_out,
        out_shape=[jax.ShapeDtypeStruct(r.shape, r.dtype) for r in results],
        in_specs=[hbm] * 5,
        out_specs=[hbm] * 5,
        scratch_shapes=[V(r.shape, r.dtype) for r in results] + [dma((5,)), dma((5,))],
        compiler_params=pltpu.CompilerParams(vmem_limit_bytes=63 << 20),
    )(*results)


def solution(mesh):
    return jax.shard_map(
        local,
        mesh=mesh,
        in_specs=(
            P(None, "island", "fsdp", None),
            P(None, "island", "fsdp", None),
            P(None, "island", "fsdp"),
            P(),
            P("island", "fsdp", None),
            P("island", "fsdp", None),
            P("fsdp", None),
            P("fsdp", None),
        ),
        out_specs=(
            P("island", "fsdp", None),
            P("island", "fsdp", None),
            P("fsdp", None),
            P("fsdp", None),
            P("island", "fsdp", None),
        ),
        check_vma=False,
    )
```
